256 devices in a mesh: grp: 2 (over z_lo), vocab: 32 (over z_hi, y, core), seq: 4 (over x).
Axes of the slice: x: 4, y: 4, z: 8 (z_hi: 4, z_lo: 2; z = z_hi * 2 + z_lo), core: 2. Of those that a mesh axis runs over, the one named last changes fastest.
Arguments:
- hidden_states: bfloat16 [2, 256, 8192], P('grp', 'seq', 'vocab'), may hold values from -128 to 127, as said below
- head_weights: bfloat16 [2, 8192, 81920], P('grp', None, ('vocab', 'seq')), may hold values from -8 to 7, as said below
- weight_scales: float32 [64, 81920], P(None, ('vocab', 'seq')), may hold values from 0.003 to 0.012
- token_scales: float32 [256], P('seq'), may hold values from 0.005 to 0.05
Outputs:
- row_grads: bfloat16 [2, 256, 8192], P('grp', 'seq', 'vocab')
- token_kl: float32 [256], replicated
The draws below stay inside these ranges and needn't reach their ends.
Inputs may be any that keep to these rules, and one draw needn't show every extreme that they name: hidden_states[1] and head_weights[1] hold whole numbers. head_weights[1] holds int4 codes.
All inputs are finite; a program needn't handle non-finite values.
Results may differ from the reference program's by a relative error of at most 0.04.
Values may be sent and summed in bfloat16 or wider, within the bound.
No kernel may reach another device: no remote copies, remote signals or barrier semaphores. Data moves between devices by JAX's collectives and lax.ppermute only.
A program may use at most 128 MiB of HBM per device.

```python
import math
import jax
import jax.numpy as jnp
from jax import lax

D = 8192
VCOL = 640
GROUP = 128
TOKENS = 256
VOCAB = 81920


def weight_column(key, index):
    column_key = jax.random.fold_in(key, index)
    first, second, third = jax.random.split(column_key, 3)
    spread = jnp.exp(jax.random.uniform(third, (), jnp.float32, math.log(0.4), math.log(4.0)))
    ref_column = jax.random.normal(first, (D,), jnp.float32) * spread / math.sqrt(D)
    codes = jax.random.randint(second, (D,), -8, 8).astype(jnp.float32)
    return (ref_column, codes)


def draw_head_weights(key, part):
    base = key

    def one(index):
        ref_column, codes = weight_column(base, index)
        return (ref_column.astype(jnp.bfloat16), codes.astype(jnp.bfloat16))
    ref_cols, code_cols = jax.lax.map(one, jnp.arange(VOCAB, dtype=jnp.int32))
    return jnp.stack([ref_cols.T, code_cols.T])


def draw_hidden_states(key, part):
    key = jax.random.fold_in(key, 7)
    first, second = jax.random.split(key, 2)
    ref_rows = jnp.clip(jax.random.normal(first, (TOKENS, D), jnp.float32) * 3.0, -18.0, 18.0)
    codes = jax.random.randint(second, (TOKENS, D), -128, 128).astype(jnp.float32)
    return jnp.stack([ref_rows, codes]).astype(jnp.bfloat16)


def block_levels(stream_key, dims, cuts, smallest, largest):
    level, own = 1.0, jax.random.fold_in(stream_key, 6)
    for position, shards_of in cuts:
        steps = jnp.exp(jax.random.uniform(jax.random.fold_in(own, position), (shards_of,), jnp.float32, smallest / len(cuts), largest / len(cuts)))
        level = level * jnp.repeat(steps, dims[position] // shards_of).reshape([-1 if axis == position else 1 for axis in range(len(dims))])
    return level


def setup_inputs(seed: int = 0) -> dict:
    arg_keys = jax.random.split(jax.random.key(seed), 5)
    hidden_states = draw_hidden_states(jax.random.fold_in(arg_keys[4], 71), 0)
    head_weights = draw_head_weights(jax.random.fold_in(arg_keys[4], 71), 0)
    weight_scales = jnp.clip(jnp.exp(math.log(0.012) - 1.3862944 * jax.random.uniform(arg_keys[2], (D // GROUP, VOCAB), jnp.float32) ** block_levels(arg_keys[2], (D // GROUP, VOCAB), ((1, 128),), -0.2, 0.2)), 0.003, 0.012)
    token_scales = jnp.clip(jnp.exp(math.log(0.05) - 2.3025851 * jax.random.uniform(arg_keys[3], (TOKENS,), jnp.float32) ** block_levels(arg_keys[3], (TOKENS,), ((0, 4),), -0.2, 0.2)), 0.005, 0.05)
    return dict(hidden_states=hidden_states, head_weights=head_weights, weight_scales=weight_scales, token_scales=token_scales)


loss_scale = 1024.0


def head_block(head_weights, weight_scales, index, model):
    start = (index * VCOL).astype(jnp.int32)
    block = lax.dynamic_slice_in_dim(head_weights[model], start, VCOL, 1)
    if model == 1:
        scales = lax.dynamic_slice_in_dim(weight_scales, start, VCOL, 1)
        grouped = block.astype(jnp.float32).reshape(D // GROUP, GROUP, VCOL) * scales[:, None, :]
        block = grouped.reshape(D, VCOL).astype(jnp.bfloat16)
    return block


def reference(hidden_states, head_weights, weight_scales, token_scales):
    blocks = VOCAB // VCOL
    indices = jnp.arange(blocks, dtype=jnp.int32)
    rows_all = [hidden_states[0],
                (hidden_states[1].astype(jnp.float32) * token_scales[:, None]).astype(jnp.bfloat16)]
    logps = []
    for model in range(2):
        rows = rows_all[model]

        def block_logits(index):
            return jnp.dot(rows, head_block(head_weights, weight_scales, index, model),
                           preferred_element_type=jnp.float32)

        logits = lax.map(block_logits, indices).transpose(1, 0, 2).reshape(TOKENS, VOCAB)
        top = jnp.max(logits, axis=1)
        lse = top + jnp.log(jnp.sum(jnp.exp(logits - top[:, None]), axis=1))
        logps.append((logits - lse[:, None]).astype(jnp.bfloat16))
    ref_lp = logps[0].astype(jnp.float32)
    quant_lp = logps[1].astype(jnp.float32)
    p_ref = jnp.exp(ref_lp)
    diff = ref_lp - quant_lp
    token_kl = jnp.sum(p_ref * diff, axis=1)
    grads = [(loss_scale * p_ref * (diff - token_kl[:, None])).astype(jnp.bfloat16),
             (loss_scale * (jnp.exp(quant_lp) - p_ref)).astype(jnp.bfloat16)]
    outputs = []
    for model in range(2):
        grad_blocks = grads[model].reshape(TOKENS, blocks, VCOL).transpose(1, 0, 2)

        def accumulate(total, item):
            index, grad_block = item
            block = head_block(head_weights, weight_scales, index, model)
            term = lax.dot_general(grad_block, block, (((1,), (1,)), ((), ())),
                                   preferred_element_type=jnp.float32)
            return total + term, None

        total, unused = lax.scan(accumulate, jnp.zeros((TOKENS, D), jnp.float32), (indices, grad_blocks))
        outputs.append(total.astype(jnp.bfloat16))
    return jnp.stack(outputs), token_kl
```

```python
import functools

import jax
import jax.numpy as jnp
from jax import lax
from jax.experimental import pallas as pl
from jax.experimental.pallas import tpu as pltpu
from jax.sharding import Mesh, PartitionSpec as P

loss_scale = 1024.0
MIB = 1024 * 1024
f32 = jnp.float32
bf16 = jnp.bfloat16

AXES = ("g", "zh", "y", "c", "x")
SIZES = (2, 4, 4, 2, 4)
GROUP = 128


def from_shift(value, axis, shift):
    n = lax.axis_size(axis)
    return lax.ppermute(value, axis, [((i + shift) % n, i) for i in range(n)])


def params(mib):
    return pltpu.CompilerParams(vmem_limit_bytes=mib * MIB)


def dequantize_kernel(place, codes, scales, out):
    core, quantized = place[1], place[2]
    for other in range(2):
        source = lax.rem(core + other, 2)
        block = codes[0, 0, source].astype(f32)
        factor = scales[0, 0, source]
        factor = jnp.where(quantized == 1, factor, 1.0)
        half = GROUP
        out[other, 0, 0, :half] = (block[:half] * factor[0:1]).astype(bf16)
        out[other, 0, 0, half:] = (block[half:] * factor[1:2]).astype(bf16)


def dequantize(place, codes, scales):
    zs, ys, cs, feats, cols = codes.shape
    return pl.pallas_call(
        dequantize_kernel,
        grid_spec=pltpu.PrefetchScalarGridSpec(
            num_scalar_prefetch=1,
            grid=(zs, ys),
            in_specs=[
                pl.BlockSpec(
                    (1, 1, cs, feats, cols),
                    lambda z, y, place: (lax.rem(z + place[0], zs), y, 0, 0, 0),
                ),
                pl.BlockSpec(
                    (1, 1, cs, feats // GROUP, cols),
                    lambda z, y, place: (lax.rem(z + place[0], zs), y, 0, 0, 0),
                ),
            ],
            out_specs=pl.BlockSpec(
                (cs, 1, 1, feats, cols), lambda z, y, place: (0, y, z, 0, 0)
            ),
        ),
        out_shape=jax.ShapeDtypeStruct((cs, ys, zs, feats, cols), bf16),
        compiler_params=params(24),
        cost_estimate=pl.CostEstimate(
            flops=zs * ys * cs * feats * cols,
            bytes_accessed=4 * zs * ys * cs * feats * cols,
            transcendentals=0,
        ),
        name="dequantize",
    )(place, codes, scales)


def first_logits_kernel(rows, weights, total):
    step = pl.program_id(0)
    part = jnp.dot(rows[0], weights[0, 0], preferred_element_type=f32)

    @pl.when(step == 0)
    def _():
        total[...] = part

    @pl.when(step > 0)
    def _():
        total[...] += part


def second_logits_kernel(rows, weights, before, total, sent):
    step = pl.program_id(0)
    part = jnp.dot(rows[0], weights[0, 0], preferred_element_type=f32)

    @pl.when(step == 0)
    def _():
        total[...] = before[...] + part

    @pl.when(step > 0)
    def _():
        total[...] += part

    @pl.when(step == pl.num_programs(0) - 1)
    def _():
        logits = total[...]
        cols = logits.shape[1]
        top = jnp.max(logits, axis=1, keepdims=True).astype(bf16)
        sent[:, :cols] = (logits - top.astype(f32)).astype(bf16)
        sent[:, cols:] = jnp.broadcast_to(top, (logits.shape[0], sent.shape[1] - cols))


def logits_part(rows, weights, half, before=None):
    ys, tokens, depth = rows.shape
    cols = weights.shape[-1]
    in_specs = [
        pl.BlockSpec((1, tokens, depth), lambda y: (y, 0, 0)),
        pl.BlockSpec((1, 1, depth, cols), lambda y: (half, y, 0, 0)),
    ]
    total_spec = pl.BlockSpec((tokens, cols), lambda y: (0, 0))
    total_shape = jax.ShapeDtypeStruct((tokens, cols), f32)
    cost = pl.CostEstimate(
        flops=2 * ys * tokens * depth * cols,
        bytes_accessed=2 * ys * depth * (cols + tokens),
        transcendentals=0,
    )
    if before is None:
        return pl.pallas_call(
            first_logits_kernel,
            grid=(ys,),
            in_specs=in_specs,
            out_specs=total_spec,
            out_shape=total_shape,
            compiler_params=params(24),
            cost_estimate=cost,
            name="logits_own",
        )(rows, weights)
    sent = (tokens, cols + 128)
    return pl.pallas_call(
        second_logits_kernel,
        grid=(ys,),
        in_specs=in_specs + [total_spec],
        out_specs=[total_spec, pl.BlockSpec(sent, lambda y: (0, 0))],
        out_shape=[total_shape, jax.ShapeDtypeStruct(sent, bf16)],
        compiler_params=params(24),
        cost_estimate=cost,
        name="logits_other",
    )(rows, weights, before)


def both_logits(quantized, own, received):
    cols = own.shape[1]
    other = received[:, :cols].astype(f32) + received[:, cols : cols + 1].astype(f32)
    return jnp.where(quantized, other, own), jnp.where(quantized, own, other)


def column_to_rows(column):
    tokens = column.shape[0]
    return jnp.transpose(jnp.broadcast_to(column, (tokens, 128)))[0:1, :]


def local_stats_kernel(place, own, received, out):
    quantized = place[2] == 1
    ref, quant = both_logits(quantized, own[...], received[...])
    ref_top = jnp.max(ref, axis=1, keepdims=True)
    ref_exp = jnp.exp(ref - ref_top)
    ref_sum = jnp.sum(ref_exp, axis=1, keepdims=True)
    ref_lse = ref_top + jnp.log(ref_sum)
    mean_diff = jnp.sum(ref_exp * (ref - quant), axis=1, keepdims=True) / ref_sum
    quant_top = jnp.max(quant, axis=1, keepdims=True)
    quant_lse = quant_top + jnp.log(
        jnp.sum(jnp.exp(quant - quant_top), axis=1, keepdims=True)
    )
    first = column_to_rows(ref_lse)
    second = column_to_rows(jnp.where(quantized, quant_lse, mean_diff))
    for i in range(first.shape[1] // 128):
        out[i : i + 1, :] = first[:, i * 128 : i * 128 + 128]
        out[2 + i : 3 + i, :] = second[:, i * 128 : i * 128 + 128]


def local_stats(place, own, received):
    return pl.pallas_call(
        local_stats_kernel,
        in_specs=[
            pl.BlockSpec(memory_space=pltpu.SMEM),
            pl.BlockSpec(memory_space=pltpu.VMEM),
            pl.BlockSpec(memory_space=pltpu.VMEM),
        ],
        out_specs=pl.BlockSpec(memory_space=pltpu.VMEM),
        out_shape=jax.ShapeDtypeStruct((4, 128), f32),
        compiler_params=params(16),
        name="local_stats",
    )(place, own, received)


def rows_to_column(row):
    return jnp.transpose(jnp.broadcast_to(row, (128, row.shape[1])))[:, 0:1]


def gradient(place, own, received, stats):
    quantized = place[2] == 1
    first = jnp.concatenate([stats[:, 0, :], stats[:, 1, :]], axis=1)
    second = jnp.concatenate([stats[:, 2, :], stats[:, 3, :]], axis=1)
    first_top = jnp.max(first, axis=0, keepdims=True)
    first_exp = jnp.exp(first - first_top)
    first_sum = jnp.sum(first_exp, axis=0, keepdims=True)
    ref_lse = first_top + jnp.log(first_sum)
    mean_diff = jnp.sum(first_exp * jnp.where(quantized, 0.0, second), axis=0, keepdims=True) / first_sum
    second_top = jnp.max(second, axis=0, keepdims=True)
    quant_lse = second_top + jnp.log(
        jnp.sum(jnp.exp(second - second_top), axis=0, keepdims=True)
    )
    kl_part = jnp.where(quantized, quant_lse, mean_diff - ref_lse)
    ref, quant = both_logits(quantized, own[...], received[...])
    p_ref = jnp.exp(ref - rows_to_column(ref_lse))
    column = rows_to_column(jnp.where(quantized, quant_lse, mean_diff))
    p_quant = jnp.exp(jnp.where(quantized, quant - column, 0.0))
    grad_ref = p_ref * (ref - quant - column)
    grad = loss_scale * jnp.where(quantized, p_quant - p_ref, grad_ref)
    return grad.astype(bf16), kl_part


def products(grad, weights, out):
    out[0] = lax.dot_general(
        grad, weights[0, 0], (((1,), (1,)), ((), ())), preferred_element_type=f32
    ).astype(bf16)


def first_products_kernel(place, own, received, stats, weights, out, grad, kl_part):
    @pl.when(pl.program_id(0) == 0)
    def _():
        grad_value, kl_value = gradient(place, own, received, stats[...])
        grad[...] = grad_value
        kl_part[...] = kl_value

    products(grad[...], weights, out)


def second_products_kernel(grad, weights, out):
    products(grad[...], weights, out)


def products_part(weights, half, grad=None, sources=None):
    halves, ys, depth, cols = weights.shape
    tokens = 256
    weight_spec = pl.BlockSpec((1, 1, depth, cols), lambda y: (half, y, 0, 0))
    out_spec = pl.BlockSpec((1, tokens, depth), lambda y: (y, 0, 0))
    out_shape = jax.ShapeDtypeStruct((ys, tokens, depth), bf16)
    grad_spec = pl.BlockSpec((tokens, cols), lambda y: (0, 0))
    cost = pl.CostEstimate(
        flops=2 * ys * tokens * depth * cols,
        bytes_accessed=2 * ys * depth * (cols + tokens),
        transcendentals=0,
    )
    if grad is not None:
        return pl.pallas_call(
            second_products_kernel,
            grid=(ys,),
            in_specs=[grad_spec, weight_spec],
            out_specs=out_spec,
            out_shape=out_shape,
            compiler_params=params(24),
            cost_estimate=cost,
            name="products_own",
        )(grad, weights)
    place, own, received, stats = sources
    whole = lambda a: pl.BlockSpec(a.shape, lambda y, n=a.ndim: (0,) * n)
    return pl.pallas_call(
        first_products_kernel,
        grid=(ys,),
        in_specs=[pl.BlockSpec(memory_space=pltpu.SMEM)]
        + [whole(own), whole(received), whole(stats), weight_spec],
        out_specs=[out_spec, grad_spec, pl.BlockSpec((1, tokens), lambda y: (0, 0))],
        out_shape=[
            out_shape,
            jax.ShapeDtypeStruct((tokens, cols), bf16),
            jax.ShapeDtypeStruct((1, tokens), f32),
        ],
        compiler_params=params(24),
        cost_estimate=cost,
        name="products_other",
    )(place, own, received, stats, weights)


def body(hidden_states, head_weights, weight_scales, token_scales):
    zs, ys, cs, xs = (lax.axis_size(a) for a in ("zh", "y", "c", "x"))
    quantized = lax.axis_index("g") == 1
    zh = lax.axis_index("zh")
    place = jnp.stack(
        [zh, lax.axis_index("c"), lax.axis_index("g")]
    ).astype(jnp.int32)
    _, local_tokens, feats = hidden_states.shape
    tokens = local_tokens * xs
    cols = head_weights.shape[2]
    row_factor = jnp.where(quantized, token_scales, 1.0)
    local_rows = (hidden_states[0].astype(f32) * row_factor[:, None]).astype(bf16)

    gathered = jnp.concatenate(
        [local_rows] + [from_shift(local_rows, "zh", k) for k in range(1, zs)], axis=1
    )
    weights = dequantize(
        place,
        head_weights.reshape(zs, ys, cs, feats, cols),
        weight_scales.reshape(zs, ys, cs, feats // GROUP, cols),
    ).reshape(cs, ys, zs * feats, cols)
    own_rows = lax.all_to_all(
        jnp.broadcast_to(gathered[None], (ys * xs,) + gathered.shape),
        ("y", "x"), 0, 0, tiled=True,
    ).reshape(ys, tokens, zs * feats)
    other_rows = from_shift(own_rows, "c", 1)
    logits = logits_part(own_rows, weights, 0)
    logits, sent = logits_part(other_rows, weights, 1, logits)
    received = from_shift(sent, "g", 1)

    stats = local_stats(place, logits, received)
    devices = zs * ys * cs * xs
    stats = lax.all_to_all(
        jnp.broadcast_to(stats[None], (devices,) + stats.shape),
        ("zh", "y", "c", "x"), 0, 0, tiled=True,
    )
    for_other, grad, kl_part = products_part(
        weights, 1, sources=(place, logits, received, stats)
    )
    token_kl = (kl_part + from_shift(kl_part, "g", 1)).reshape(tokens)
    from_other = from_shift(for_other, "c", 1)
    kept = products_part(weights, 0, grad=grad)
    chip = (kept.astype(f32) + from_other.astype(f32)).astype(bf16)
    parts = lax.all_to_all(
        chip.reshape(ys * xs, local_tokens, zs * feats), ("y", "x"), 0, 0, tiled=True
    )
    plane = jnp.sum(parts.astype(f32), axis=0).astype(bf16)
    blocks = plane.reshape(local_tokens, zs, feats).transpose(1, 0, 2)
    blocks = lax.dynamic_slice_in_dim(
        jnp.concatenate([blocks, blocks]), lax.rem(zs - zh, zs), zs, 0
    )
    blocks = lax.all_to_all(blocks, "zh", 0, 0, tiled=True)
    result = jnp.sum(blocks.astype(f32), axis=0).astype(bf16)
    return (result[None], token_kl)


def solution(mesh):
    fine = Mesh(mesh.devices.reshape(SIZES), AXES)
    vocab = ("zh", "y", "c")
    columns = vocab + ("x",)
    return jax.shard_map(
        body,
        mesh=fine,
        in_specs=(P("g", "x", vocab), P("g", None, columns), P(None, columns), P("x")),
        out_specs=(P("g", "x", vocab), P()),
        check_vma=False,
    )
```

```python
import functools

import jax
import jax.numpy as jnp
from jax import lax
from jax.experimental import pallas as pl
from jax.experimental.pallas import tpu as pltpu
from jax.sharding import Mesh, PartitionSpec as P

loss_scale = 1024.0
MIB = 1024 * 1024
GROUP = 128
f32 = jnp.float32
bf16 = jnp.bfloat16

AXES = ("g", "zh", "y", "c", "x")
SIZES = (2, 4, 4, 2, 4)


def from_shift(value, axis, shift):
    n = lax.axis_size(axis)
    return lax.ppermute(value, axis, [((i + shift) % n, i) for i in range(n)])


def gather_ring(value, axis, zero):
    following = from_shift(value, axis, 1)
    previous = from_shift(value, axis, 3)
    half = value.shape[0] // 2
    opposite = (
        from_shift(following[:half] + zero, axis, 1),
        from_shift(previous[half:] + zero, axis, 3),
    )
    return value, following, previous, opposite


def total(*parts):
    return sum(part.astype(f32) for part in parts).astype(bf16)


def params(mib):
    return pltpu.CompilerParams(vmem_limit_bytes=mib * MIB)


def pick(step, values):
    value = jnp.int32(values[0])
    for i, other in enumerate(values[1:], 1):
        value = jnp.where(step == i, jnp.int32(other), value)
    return value


def dequantize_kernel(place, codes, scales, out, ready):
    core, quantized = place[1], place[2]
    for other in range(2):
        source = lax.rem(core + other, 2)
        block = codes[0, 0, source].astype(f32)
        factor = scales[0, 0, source]
        factor = jnp.where(quantized == 1, factor, 1.0)
        half = GROUP
        out[other, 0, 0, :half] = (block[:half] * factor[0:1]).astype(bf16)
        out[other, 0, 0, half:] = (block[half:] * factor[1:2]).astype(bf16)
    ready[...] = jnp.zeros(ready.shape, ready.dtype)


def dequantize(place, codes, scales):
    zs, ys, cs, feats, cols = codes.shape
    where = lambda z, y, place: (z, lax.rem(y + place[0], ys), 0, 0, 0)
    return pl.pallas_call(
        dequantize_kernel,
        grid_spec=pltpu.PrefetchScalarGridSpec(
            num_scalar_prefetch=1,
            grid=(zs, ys),
            in_specs=[
                pl.BlockSpec((1, 1, cs, feats, cols), where),
                pl.BlockSpec((1, 1, cs, feats // GROUP, cols), where),
            ],
            out_specs=[
                pl.BlockSpec((cs, 1, 1, feats, cols), lambda z, y, place: (0, y, z, 0, 0)),
                pl.BlockSpec((16, 128), lambda z, y, place: (0, 0)),
            ],
        ),
        out_shape=[
            jax.ShapeDtypeStruct((cs, ys, zs, feats, cols), bf16),
            jax.ShapeDtypeStruct((16, 128), bf16),
        ],
        compiler_params=params(24),
        cost_estimate=pl.CostEstimate(
            flops=zs * ys * cs * feats * cols,
            bytes_accessed=4 * zs * ys * cs * feats * cols,
            transcendentals=0,
        ),
        name="dequantize",
    )(place, codes, scales)


def column_to_row(column):
    tokens = column.shape[0]
    return jnp.transpose(jnp.broadcast_to(column, (tokens, 128)))[0:1, :]


def row_to_column(row):
    return jnp.transpose(jnp.broadcast_to(row, (128, row.shape[1])))[:, 0:1]


def logits_kernel(counts, resumed, last, *refs):
    rows, refs = refs[: sum(counts)], refs[sum(counts) :]
    weights, refs = refs[0], refs[1:]
    if resumed:
        before, refs = refs[0], refs[1:]
    logits, refs = refs[0], refs[1:]
    step = pl.program_id(0)
    start = 0
    for i, count in enumerate(counts):
        parts = rows[start : start + count]
        start += count

        @pl.when(step == i)
        def _(i=i, parts=parts):
            block = jnp.concatenate([part[...] for part in parts], axis=0)
            value = jnp.dot(block, weights[0, 0], preferred_element_type=f32)
            if i:
                value = logits[...] + value
            elif resumed:
                value = before[...] + value
            logits[...] = value
            if last and i == len(counts) - 1:
                sent = refs[0]
                tokens, cols = value.shape
                top = jnp.max(value, axis=1, keepdims=True).astype(bf16).astype(f32)
                sent[:tokens] = (value - top).astype(bf16)
                extra = sent.shape[0] - tokens
                row = jnp.broadcast_to(column_to_row(top), (extra, tokens))
                sent[tokens:, :tokens] = row.astype(bf16)
                sent[tokens:, tokens:] = jnp.zeros((extra, cols - tokens), bf16)


def logits_part(blocks, weights, before=None, last=False):
    _, _, depth, cols = weights.shape
    tokens = sum(part.shape[0] for part in blocks[0][2])
    halves = [half for half, _, _ in blocks]
    places = [place for _, place, _ in blocks]
    rows = [part for _, _, parts in blocks for part in parts]
    whole = lambda shape: pl.BlockSpec(shape, lambda s: (0, 0))
    in_specs = [whole(part.shape) for part in rows] + [
        pl.BlockSpec((1, 1, depth, cols), lambda s: (pick(s, halves), pick(s, places), 0, 0))
    ]
    operands = rows + [weights]
    if before is not None:
        in_specs.append(whole((tokens, cols)))
        operands.append(before)
    out_specs = [whole((tokens, cols))]
    out_shape = [jax.ShapeDtypeStruct((tokens, cols), f32)]
    if last:
        out_specs.append(whole((tokens + 16, cols)))
        out_shape.append(jax.ShapeDtypeStruct((tokens + 16, cols), bf16))
    counts = [len(parts) for _, _, parts in blocks]
    return pl.pallas_call(
        functools.partial(logits_kernel, counts, before is not None, last),
        grid=(len(blocks),),
        in_specs=in_specs,
        out_specs=out_specs,
        out_shape=out_shape,
        compiler_params=params(24),
        cost_estimate=pl.CostEstimate(
            flops=2 * len(blocks) * tokens * depth * cols,
            bytes_accessed=2 * len(blocks) * depth * (cols + tokens),
            transcendentals=0,
        ),
        name="logits",
    )(*operands)


def both_logits(quantized, own, received):
    tokens = own.shape[0]
    top = row_to_column(received[tokens : tokens + 1, :tokens].astype(f32))
    other = received[:tokens, :].astype(f32) + top
    return jnp.where(quantized, other, own), jnp.where(quantized, own, other)


def local_stats_kernel(place, own, received, out):
    quantized = place[2] == 1
    ref, quant = both_logits(quantized, own[...], received[...])
    ref_top = jnp.max(ref, axis=1, keepdims=True)
    ref_exp = jnp.exp(ref - ref_top)
    ref_sum = jnp.sum(ref_exp, axis=1, keepdims=True)
    ref_lse = ref_top + jnp.log(ref_sum)
    mean_diff = jnp.sum(ref_exp * (ref - quant), axis=1, keepdims=True) / ref_sum
    quant_top = jnp.max(quant, axis=1, keepdims=True)
    quant_lse = quant_top + jnp.log(
        jnp.sum(jnp.exp(quant - quant_top), axis=1, keepdims=True)
    )
    first = column_to_row(ref_lse)
    second = column_to_row(jnp.where(quantized, quant_lse, mean_diff))
    for i in range(first.shape[1] // 128):
        out[i : i + 1, :] = first[:, i * 128 : i * 128 + 128]
        out[2 + i : 3 + i, :] = second[:, i * 128 : i * 128 + 128]


def local_stats(place, own, received):
    return pl.pallas_call(
        local_stats_kernel,
        in_specs=[
            pl.BlockSpec(memory_space=pltpu.SMEM),
            pl.BlockSpec(memory_space=pltpu.VMEM),
            pl.BlockSpec(memory_space=pltpu.VMEM),
        ],
        out_specs=pl.BlockSpec(memory_space=pltpu.VMEM),
        out_shape=jax.ShapeDtypeStruct((4, 128), f32),
        compiler_params=params(16),
        name="local_stats",
    )(place, own, received)


def gradient(place, own, received, stats):
    quantized = place[2] == 1
    first = jnp.concatenate([stats[:, 0, :], stats[:, 1, :]], axis=1)
    second = jnp.concatenate([stats[:, 2, :], stats[:, 3, :]], axis=1)
    first_top = jnp.max(first, axis=0, keepdims=True)
    first_exp = jnp.exp(first - first_top)
    first_sum = jnp.sum(first_exp, axis=0, keepdims=True)
    ref_lse = first_top + jnp.log(first_sum)
    mean_diff = (
        jnp.sum(first_exp * jnp.where(quantized, 0.0, second), axis=0, keepdims=True)
        / first_sum
    )
    second_top = jnp.max(second, axis=0, keepdims=True)
    quant_lse = second_top + jnp.log(
        jnp.sum(jnp.exp(second - second_top), axis=0, keepdims=True)
    )
    kl_part = jnp.where(quantized, quant_lse, mean_diff - ref_lse)
    ref, quant = both_logits(quantized, own[...], received[...])
    p_ref = jnp.exp(ref - row_to_column(ref_lse))
    column = row_to_column(jnp.where(quantized, quant_lse, mean_diff))
    p_quant = jnp.exp(jnp.where(quantized, quant - column, 0.0))
    grad_ref = p_ref * (ref - quant - column)
    grad = loss_scale * jnp.where(quantized, p_quant - p_ref, grad_ref)
    return grad.astype(bf16), kl_part


def products(grad, weights, outs):
    value = lax.dot_general(
        grad, weights[0, 0], (((1,), (1,)), ((), ())), preferred_element_type=f32
    ).astype(bf16)
    for i, out in enumerate(outs):

        @pl.when(pl.program_id(0) == i)
        def _(out=out):
            out[...] = value


def first_products_kernel(place, own, received, stats, weights, *outs):
    *outs, grad, kl_part = outs

    @pl.when(pl.program_id(0) == 0)
    def _():
        grad_value, kl_value = gradient(place, own, received, stats[...])
        grad[...] = grad_value
        kl_part[...] = kl_value

    products(grad[...], weights, outs)


def more_products_kernel(grad, weights, *outs):
    products(grad[...], weights, outs)


def products_part(blocks, weights, tokens, grad=None, sources=None):
    _, _, depth, cols = weights.shape
    halves = [half for half, _ in blocks]
    places = [place for _, place in blocks]
    whole = lambda shape: pl.BlockSpec(shape, lambda s, n=len(shape): (0,) * n)
    weight_spec = pl.BlockSpec(
        (1, 1, depth, cols), lambda s: (pick(s, halves), pick(s, places), 0, 0)
    )
    out_specs = [whole((tokens, depth))] * len(blocks)
    out_shape = [jax.ShapeDtypeStruct((tokens, depth), bf16)] * len(blocks)
    cost = pl.CostEstimate(
        flops=2 * len(blocks) * tokens * depth * cols,
        bytes_accessed=2 * len(blocks) * depth * (cols + tokens),
        transcendentals=0,
    )
    if grad is not None:
        return pl.pallas_call(
            more_products_kernel,
            grid=(len(blocks),),
            in_specs=[whole(grad.shape), weight_spec],
            out_specs=out_specs,
            out_shape=out_shape,
            compiler_params=params(24),
            cost_estimate=cost,
            name="products",
        )(grad, weights)
    place, own, received, stats = sources
    return pl.pallas_call(
        first_products_kernel,
        grid=(len(blocks),),
        in_specs=[pl.BlockSpec(memory_space=pltpu.SMEM)]
        + [whole(own.shape), whole(received.shape), whole(stats.shape), weight_spec],
        out_specs=out_specs + [whole((tokens, cols)), whole((1, tokens))],
        out_shape=out_shape
        + [
            jax.ShapeDtypeStruct((tokens, cols), bf16),
            jax.ShapeDtypeStruct((1, tokens), f32),
        ],
        compiler_params=params(24),
        cost_estimate=cost,
        name="gradient_products",
    )(place, own, received, stats, weights)


def body(hidden_states, head_weights, weight_scales, token_scales):
    zs, ys, cs, xs = (lax.axis_size(a) for a in ("zh", "y", "c", "x"))
    quantized = lax.axis_index("g") == 1
    _, local_tokens, feats = hidden_states.shape
    tokens = local_tokens * xs
    cols = head_weights.shape[2]
    place = jnp.stack([lax.axis_index(a) for a in ("y", "c", "g")]).astype(jnp.int32)
    row_factor = jnp.where(quantized, token_scales, 1.0)
    local_rows = (hidden_states[0].astype(f32) * row_factor[:, None]).astype(bf16)
    weights, ready = dequantize(
        place,
        head_weights.reshape(zs, ys, cs, feats, cols),
        weight_scales.reshape(zs, ys, cs, feats // GROUP, cols),
    )
    weights = weights.reshape(cs, ys, zs * feats, cols)

    rows = lax.all_to_all(
        jnp.broadcast_to(local_rows[None], (zs * xs,) + local_rows.shape),
        ("zh", "x"), 0, 0, tiled=True,
    ).reshape(zs, tokens, feats)
    rows = jnp.concatenate([rows[z] for z in range(zs)], axis=1)
    own, following, previous, opposite = gather_ring(rows, "y", ready[0, 0])
    near = [(0, (own,)), (1, (following,)), (3, (previous,))]
    across = lambda parts: tuple(from_shift(part, "c", 1) for part in parts)
    logits, = logits_part([(0, p, parts) for p, parts in near], weights)
    logits, = logits_part([(1, p, across(parts)) for p, parts in near], weights, logits)
    opposite, logits = lax.optimization_barrier((opposite, logits))
    logits, sent = logits_part(
        [(0, 2, opposite), (1, 2, across(opposite))], weights, logits, last=True
    )
    received = from_shift(sent, "g", 1)

    stats = local_stats(place, logits, received)
    devices = zs * ys * cs * xs
    stats = lax.all_to_all(
        jnp.broadcast_to(stats[None], (devices,) + stats.shape),
        ("zh", "y", "c", "x"), 0, 0, tiled=True,
    )

    sent_2, kept_2, grad, kl_part = products_part(
        [(1, 2), (0, 2)], weights, tokens, sources=(place, logits, received, stats)
    )
    came_2 = from_shift(sent_2, "c", 1)
    sent_1, sent_3, sent_0 = products_part(
        [(1, 1), (1, 3), (1, 0)], weights, tokens, grad=grad
    )
    opposite = total(kept_2, came_2)
    came_1, came_3, came_0 = (from_shift(a, "c", 1) for a in (sent_1, sent_3, sent_0))
    kept_1, kept_3, kept_0 = products_part(
        [(0, 1), (0, 3), (0, 0)], weights, tokens, grad=grad
    )
    half = tokens // 2
    low = from_shift(opposite[:half], "y", 3)
    high = from_shift(opposite[half:], "y", 1)
    following = jnp.concatenate(
        [total(kept_1[:half], came_1[:half], low), total(kept_1[half:], came_1[half:])]
    )
    previous = jnp.concatenate(
        [total(kept_3[:half], came_3[:half]), total(kept_3[half:], came_3[half:], high)]
    )
    kl_other = from_shift(kl_part, "g", 1)
    own = total(
        kept_0, came_0, from_shift(following, "y", 3), from_shift(previous, "y", 1)
    )
    own, kl_other = lax.optimization_barrier((own, kl_other))
    own = jnp.concatenate([own[:, z * feats : (z + 1) * feats] for z in range(zs)])
    own = lax.all_to_all(
        own.reshape(zs * xs, local_tokens, feats), ("zh", "x"), 0, 0, tiled=True
    )
    own = jnp.sum(own.astype(f32), axis=0).astype(bf16)
    return (own[None], (kl_part + kl_other).reshape(tokens))


def solution(mesh):
    fine = Mesh(mesh.devices.reshape(SIZES), AXES)
    vocab = ("zh", "y", "c")
    columns = vocab + ("x",)
    return jax.shard_map(
        body,
        mesh=fine,
        in_specs=(P("g", "x", vocab), P("g", None, columns), P(None, columns), P("x")),
        out_specs=(P("g", "x", vocab), P()),
        check_vma=False,
    )
```

```python
import functools

import jax
import jax.numpy as jnp
from jax import lax
from jax.experimental import pallas as pl
from jax.experimental.pallas import tpu as pltpu
from jax.sharding import Mesh, PartitionSpec as P

loss_scale = 1024.0
MIB = 1024 * 1024
GROUP = 128
f32 = jnp.float32
bf16 = jnp.bfloat16

AXES = ("g", "zh", "y", "c", "x")
SIZES = (2, 4, 4, 2, 4)


def from_shift(value, axis, shift):
    n = lax.axis_size(axis)
    return lax.ppermute(value, axis, [((i + shift) % n, i) for i in range(n)])


def gather_ring(value, axis, zero):
    following = from_shift(value, axis, 1)
    previous = from_shift(value, axis, 3)
    half = value.shape[0] // 2
    opposite = (
        from_shift(following[:half] + zero, axis, 1),
        from_shift(previous[half:] + zero, axis, 3),
    )
    return value, following, previous, opposite


def total(*parts):
    return sum(part.astype(f32) for part in parts).astype(bf16)


def params(mib):
    return pltpu.CompilerParams(vmem_limit_bytes=mib * MIB)


def pick(step, values):
    value = jnp.int32(values[0])
    for i, other in enumerate(values[1:], 1):
        value = jnp.where(step == i, jnp.int32(other), value)
    return value


def dequantize_kernel(place, codes, scales, out, ready):
    core, quantized = place[1], place[2]
    for other in range(2):
        source = lax.rem(core + other, 2)
        block = codes[0, 0, source].astype(f32)
        factor = scales[0, 0, source]
        factor = jnp.where(quantized == 1, factor, 1.0)
        half = GROUP
        out[other, 0, 0, :half] = (block[:half] * factor[0:1]).astype(bf16)
        out[other, 0, 0, half:] = (block[half:] * factor[1:2]).astype(bf16)
    ready[...] = jnp.zeros(ready.shape, ready.dtype)


def dequantize(place, codes, scales):
    zs, ys, cs, feats, cols = codes.shape
    where = lambda z, y, place: (z, lax.rem(y + place[0], ys), 0, 0, 0)
    return pl.pallas_call(
        dequantize_kernel,
        grid_spec=pltpu.PrefetchScalarGridSpec(
            num_scalar_prefetch=1,
            grid=(zs, ys),
            in_specs=[
                pl.BlockSpec((1, 1, cs, feats, cols), where),
                pl.BlockSpec((1, 1, cs, feats // GROUP, cols), where),
            ],
            out_specs=[
                pl.BlockSpec((cs, 1, 1, feats, cols), lambda z, y, place: (0, y, z, 0, 0)),
                pl.BlockSpec((16, 128), lambda z, y, place: (0, 0)),
            ],
        ),
        out_shape=[
            jax.ShapeDtypeStruct((cs, ys, zs, feats, cols), bf16),
            jax.ShapeDtypeStruct((16, 128), bf16),
        ],
        compiler_params=params(24),
        cost_estimate=pl.CostEstimate(
            flops=zs * ys * cs * feats * cols,
            bytes_accessed=4 * zs * ys * cs * feats * cols,
            transcendentals=0,
        ),
        name="dequantize",
    )(place, codes, scales)


def column_to_row(column):
    tokens = column.shape[0]
    return jnp.transpose(jnp.broadcast_to(column, (tokens, 128)))[0:1, :]


def row_to_column(row):
    return jnp.transpose(jnp.broadcast_to(row, (128, row.shape[1])))[:, 0:1]


def logits_kernel(counts, resumed, last, *refs):
    rows, refs = refs[: sum(counts)], refs[sum(counts) :]
    weights, refs = refs[0], refs[1:]
    if resumed:
        before, refs = refs[0], refs[1:]
    logits, refs = refs[0], refs[1:]
    step = pl.program_id(0)
    start = 0
    for i, count in enumerate(counts):
        parts = rows[start : start + count]
        start += count

        @pl.when(step == i)
        def _(i=i, parts=parts):
            block = jnp.concatenate([part[...] for part in parts], axis=0)
            value = jnp.dot(block, weights[0, 0], preferred_element_type=f32)
            if i:
                value = logits[...] + value
            elif resumed:
                value = before[...] + value
            logits[...] = value
            if last and i == len(counts) - 1:
                sent = refs[0]
                tokens, cols = value.shape
                top = jnp.max(value, axis=1, keepdims=True).astype(bf16).astype(f32)
                sent[:tokens] = (value - top).astype(bf16)
                extra = sent.shape[0] - tokens
                row = jnp.broadcast_to(column_to_row(top), (extra, tokens))
                sent[tokens:, :tokens] = row.astype(bf16)
                sent[tokens:, tokens:] = jnp.zeros((extra, cols - tokens), bf16)


def logits_part(blocks, weights, before=None, last=False):
    _, _, depth, cols = weights.shape
    tokens = sum(part.shape[0] for part in blocks[0][2])
    halves = [half for half, _, _ in blocks]
    places = [place for _, place, _ in blocks]
    rows = [part for _, _, parts in blocks for part in parts]
    whole = lambda shape: pl.BlockSpec(shape, lambda s: (0, 0))
    in_specs = [whole(part.shape) for part in rows] + [
        pl.BlockSpec((1, 1, depth, cols), lambda s: (pick(s, halves), pick(s, places), 0, 0))
    ]
    operands = rows + [weights]
    if before is not None:
        in_specs.append(whole((tokens, cols)))
        operands.append(before)
    out_specs = [whole((tokens, cols))]
    out_shape = [jax.ShapeDtypeStruct((tokens, cols), f32)]
    if last:
        out_specs.append(whole((tokens + 16, cols)))
        out_shape.append(jax.ShapeDtypeStruct((tokens + 16, cols), bf16))
    counts = [len(parts) for _, _, parts in blocks]
    return pl.pallas_call(
        functools.partial(logits_kernel, counts, before is not None, last),
        grid=(len(blocks),),
        in_specs=in_specs,
        out_specs=out_specs,
        out_shape=out_shape,
        compiler_params=params(24),
        cost_estimate=pl.CostEstimate(
            flops=2 * len(blocks) * tokens * depth * cols,
            bytes_accessed=2 * len(blocks) * depth * (cols + tokens),
            transcendentals=0,
        ),
        name="logits",
    )(*operands)


def both_logits(quantized, own, received):
    tokens = own.shape[0]
    top = row_to_column(received[tokens : tokens + 1, :tokens].astype(f32))
    other = received[:tokens, :].astype(f32) + top
    return jnp.where(quantized, other, own), jnp.where(quantized, own, other)


def local_stats_kernel(place, own, received, out):
    quantized = place[2] == 1
    ref, quant = both_logits(quantized, own[...], received[...])
    ref_top = jnp.max(ref, axis=1, keepdims=True)
    ref_exp = jnp.exp(ref - ref_top)
    ref_sum = jnp.sum(ref_exp, axis=1, keepdims=True)
    ref_lse = ref_top + jnp.log(ref_sum)
    mean_diff = jnp.sum(ref_exp * (ref - quant), axis=1, keepdims=True) / ref_sum
    quant_top = jnp.max(quant, axis=1, keepdims=True)
    quant_lse = quant_top + jnp.log(
        jnp.sum(jnp.exp(quant - quant_top), axis=1, keepdims=True)
    )
    first = column_to_row(ref_lse)
    second = column_to_row(jnp.where(quantized, quant_lse, mean_diff))
    for i in range(first.shape[1] // 128):
        out[i : i + 1, :] = first[:, i * 128 : i * 128 + 128]
        out[2 + i : 3 + i, :] = second[:, i * 128 : i * 128 + 128]


def local_stats(place, own, received):
    return pl.pallas_call(
        local_stats_kernel,
        in_specs=[
            pl.BlockSpec(memory_space=pltpu.SMEM),
            pl.BlockSpec(memory_space=pltpu.VMEM),
            pl.BlockSpec(memory_space=pltpu.VMEM),
        ],
        out_specs=pl.BlockSpec(memory_space=pltpu.VMEM),
        out_shape=jax.ShapeDtypeStruct((4, 128), f32),
        compiler_params=params(16),
        name="local_stats",
    )(place, own, received)


def gradient(place, own, received, stats):
    quantized = place[2] == 1
    first = jnp.concatenate([stats[:, 0, :], stats[:, 1, :]], axis=1)
    second = jnp.concatenate([stats[:, 2, :], stats[:, 3, :]], axis=1)
    first_top = jnp.max(first, axis=0, keepdims=True)
    first_exp = jnp.exp(first - first_top)
    first_sum = jnp.sum(first_exp, axis=0, keepdims=True)
    ref_lse = first_top + jnp.log(first_sum)
    mean_diff = (
        jnp.sum(first_exp * jnp.where(quantized, 0.0, second), axis=0, keepdims=True)
        / first_sum
    )
    second_top = jnp.max(second, axis=0, keepdims=True)
    quant_lse = second_top + jnp.log(
        jnp.sum(jnp.exp(second - second_top), axis=0, keepdims=True)
    )
    kl_part = jnp.where(quantized, quant_lse, mean_diff - ref_lse)
    ref, quant = both_logits(quantized, own[...], received[...])
    p_ref = jnp.exp(ref - row_to_column(ref_lse))
    column = row_to_column(jnp.where(quantized, quant_lse, mean_diff))
    p_quant = jnp.exp(jnp.where(quantized, quant - column, 0.0))
    grad_ref = p_ref * (ref - quant - column)
    grad = loss_scale * jnp.where(quantized, p_quant - p_ref, grad_ref)
    return grad.astype(bf16), kl_part


def products(grad, weights, outs):
    value = lax.dot_general(
        grad, weights[0, 0], (((1,), (1,)), ((), ())), preferred_element_type=f32
    ).astype(bf16)
    for i, out in enumerate(outs):

        @pl.when(pl.program_id(0) == i)
        def _(out=out):
            out[...] = value


def first_products_kernel(place, own, received, stats, weights, *outs):
    *outs, grad, kl_part = outs

    @pl.when(pl.program_id(0) == 0)
    def _():
        grad_value, kl_value = gradient(place, own, received, stats[...])
        grad[...] = grad_value
        kl_part[...] = kl_value

    products(grad[...], weights, outs)


def more_products_kernel(grad, weights, *outs):
    products(grad[...], weights, outs)


def summed_products_kernel(grad, weights, *refs):
    blocks = len(refs) // 3
    value = lax.dot_general(
        grad[...], weights[0, 0], (((1,), (1,)), ((), ())), preferred_element_type=f32
    )
    for i in range(blocks):
        came, low, high = refs[i], refs[blocks + 2 * i], refs[blocks + 2 * i + 1]

        @pl.when(pl.program_id(0) == i)
        def _(came=came, low=low, high=high):
            half = low.shape[0]
            low[...] = (value[:half] + came[:half].astype(f32)).astype(bf16)
            high[...] = (value[half:] + came[half:].astype(f32)).astype(bf16)


def products_part(blocks, weights, tokens, grad=None, sources=None, came=()):
    _, _, depth, cols = weights.shape
    halves = [half for half, _ in blocks]
    places = [place for _, place in blocks]
    whole = lambda shape: pl.BlockSpec(shape, lambda s, n=len(shape): (0,) * n)
    weight_spec = pl.BlockSpec(
        (1, 1, depth, cols), lambda s: (pick(s, halves), pick(s, places), 0, 0)
    )
    out_specs = [whole((tokens, depth))] * len(blocks)
    out_shape = [jax.ShapeDtypeStruct((tokens, depth), bf16)] * len(blocks)
    cost = pl.CostEstimate(
        flops=2 * len(blocks) * tokens * depth * cols,
        bytes_accessed=2 * len(blocks) * depth * (cols + tokens),
        transcendentals=0,
    )
    if came:
        part = (tokens // 2, depth)
        return pl.pallas_call(
            summed_products_kernel,
            grid=(len(blocks),),
            in_specs=[whole(grad.shape), weight_spec] + [whole(a.shape) for a in came],
            out_specs=[whole(part)] * (2 * len(blocks)),
            out_shape=[jax.ShapeDtypeStruct(part, bf16)] * (2 * len(blocks)),
            compiler_params=params(24),
            cost_estimate=cost,
            name="summed_products",
        )(grad, weights, *came)
    if grad is not None:
        return pl.pallas_call(
            more_products_kernel,
            grid=(len(blocks),),
            in_specs=[whole(grad.shape), weight_spec],
            out_specs=out_specs,
            out_shape=out_shape,
            compiler_params=params(24),
            cost_estimate=cost,
            name="products",
        )(grad, weights)
    place, own, received, stats = sources
    return pl.pallas_call(
        first_products_kernel,
        grid=(len(blocks),),
        in_specs=[pl.BlockSpec(memory_space=pltpu.SMEM)]
        + [whole(own.shape), whole(received.shape), whole(stats.shape), weight_spec],
        out_specs=out_specs + [whole((tokens, cols)), whole((1, tokens))],
        out_shape=out_shape
        + [
            jax.ShapeDtypeStruct((tokens, cols), bf16),
            jax.ShapeDtypeStruct((1, tokens), f32),
        ],
        compiler_params=params(24),
        cost_estimate=cost,
        name="gradient_products",
    )(place, own, received, stats, weights)


def body(hidden_states, head_weights, weight_scales, token_scales):
    zs, ys, cs, xs = (lax.axis_size(a) for a in ("zh", "y", "c", "x"))
    quantized = lax.axis_index("g") == 1
    _, local_tokens, feats = hidden_states.shape
    tokens = local_tokens * xs
    cols = head_weights.shape[2]
    place = jnp.stack([lax.axis_index(a) for a in ("y", "c", "g")]).astype(jnp.int32)
    row_factor = jnp.where(quantized, token_scales, 1.0)
    local_rows = (hidden_states[0].astype(f32) * row_factor[:, None]).astype(bf16)
    weights, ready = dequantize(
        place,
        head_weights.reshape(zs, ys, cs, feats, cols),
        weight_scales.reshape(zs, ys, cs, feats // GROUP, cols),
    )
    weights = weights.reshape(cs, ys, zs * feats, cols)

    rows = lax.all_to_all(
        jnp.broadcast_to(local_rows[None], (zs * xs,) + local_rows.shape),
        ("zh", "x"), 0, 0, tiled=True,
    ).reshape(zs, tokens, feats)
    rows = jnp.concatenate([rows[z] for z in range(zs)], axis=1)
    own, following, previous, opposite = gather_ring(rows, "y", ready[0, 0])
    near = [(0, (own,)), (1, (following,)), (3, (previous,))]
    across = lambda parts: tuple(from_shift(part, "c", 1) for part in parts)
    logits, = logits_part([(0, p, parts) for p, parts in near], weights)
    logits, = logits_part([(1, p, across(parts)) for p, parts in near], weights, logits)
    opposite, logits = lax.optimization_barrier((opposite, logits))
    logits, sent = logits_part(
        [(0, 2, opposite), (1, 2, across(opposite))], weights, logits, last=True
    )
    received = from_shift(sent, "g", 1)

    stats = local_stats(place, logits, received)
    devices = zs * ys * cs * xs
    stats = lax.all_to_all(
        jnp.broadcast_to(stats[None], (devices,) + stats.shape),
        ("zh", "y", "c", "x"), 0, 0, tiled=True,
    )

    sent_2, kept_2, grad, kl_part = products_part(
        [(1, 2), (0, 2)], weights, tokens, sources=(place, logits, received, stats)
    )
    came_2 = from_shift(sent_2, "c", 1)
    sent_1, sent_3, sent_0 = products_part(
        [(1, 1), (1, 3), (1, 0)], weights, tokens, grad=grad
    )
    opposite = total(kept_2, came_2)
    came_1, came_3, came_0 = (from_shift(a, "c", 1) for a in (sent_1, sent_3, sent_0))
    low_1, high_1, low_3, high_3, low_0, high_0 = products_part(
        [(0, 1), (0, 3), (0, 0)], weights, tokens, grad=grad, came=(came_1, came_3, came_0)
    )
    half = tokens // 2
    low = from_shift(opposite[:half], "y", 3)
    high = from_shift(opposite[half:], "y", 1)
    high_1 = from_shift(high_1, "y", 3)
    low_3 = from_shift(low_3, "y", 1)
    low_1 = from_shift(total(low_1, low), "y", 3)
    high_3 = from_shift(total(high_3, high), "y", 1)
    kl_other = from_shift(kl_part, "g", 1)
    own = jnp.concatenate([total(low_0, low_1, low_3), total(high_0, high_1, high_3)])
    own, kl_other = lax.optimization_barrier((own, kl_other))
    own = jnp.concatenate([own[:, z * feats : (z + 1) * feats] for z in range(zs)])
    own = lax.all_to_all(
        own.reshape(zs * xs, local_tokens, feats), ("zh", "x"), 0, 0, tiled=True
    )
    own = jnp.sum(own.astype(f32), axis=0).astype(bf16)
    return (own[None], (kl_part + kl_other).reshape(tokens))


def solution(mesh):
    fine = Mesh(mesh.devices.reshape(SIZES), AXES)
    vocab = ("zh", "y", "c")
    columns = vocab + ("x",)
    return jax.shard_map(
        body,
        mesh=fine,
        in_specs=(P("g", "x", vocab), P("g", None, columns), P(None, columns), P("x")),
        out_specs=(P("g", "x", vocab), P()),
        check_vma=False,
    )
```
